256 devices in a mesh: row: 32 (over z, x_lo, core), rep: 8 (over x_hi, y).
Axes of the slice: x: 4 (x_hi: 2, x_lo: 2; x = x_hi * 2 + x_lo), y: 4, z: 8, core: 2. Of those that a mesh axis runs over, the one named last changes fastest.
Arguments:
- features: bfloat16 [65536, 128], P(('row', 'rep')), may hold values from -6 to 6
- tile_values: bfloat16 [65536, 128, 128], P(('row', 'rep')), may hold values from 0 to 100, as said below
- tile_rows: int32 [256, 256], P(('row', 'rep')), may hold values from 0 to 15
- tile_cols: int32 [256, 256], P(('row', 'rep')), may hold values from 0 to 1
- tile_count: int32 [256, 32], P(('row', 'rep')), may hold values from 1 to 8, as said below
- weight: bfloat16 [128, 256], replicated, may hold values from -6 to 6
- bias: float32 [256], replicated, may hold values from -3 to 3
- cotangent: bfloat16 [65536, 256], P(('row', 'rep')), may hold values from -6 to 6
Outputs:
- hidden_out: bfloat16 [65536, 256], P(('row', 'rep'))
- grad_features: bfloat16 [65536, 128], P(('row', 'rep'))
- grad_weight: float32 [128, 256], replicated
The draws below stay inside these ranges and needn't reach their ends.
Inputs may be any that keep to these rules, and one draw needn't show every extreme that they name: `tile_values`: nonnegative edge weights, zero where a tile has no edge. `tile_count`: in every device some source block has all 8 slots live.
All inputs are finite; a program needn't handle non-finite values.
Results may differ from the reference program's by a relative error of at most 0.012.
Values may be sent and summed in bfloat16 or wider, within the bound.
No kernel may reach another device: no remote copies, remote signals or barrier semaphores. Data moves between devices by JAX's collectives and lax.ppermute only.
A program may use at most 128 MiB of HBM per device.

```python
import jax
import jax.numpy as jnp
from jax import lax

F_IN = 128
HID = 256
TILE = 128
SLOTS = 8
NODE_DEV = 2048
NODES = 65536
NODE_SUB = 256
N_ROW = 32
N_REP = 8


def draw_tile_values(key, part):
    key = jax.random.fold_in(key, 11)
    key_keep, key_size = jax.random.split(key, 2)
    shape = (N_ROW * N_REP * N_ROW * SLOTS, TILE, TILE)
    keep = (jax.random.uniform(key_keep, shape, jnp.float32) < 0.25).astype(jnp.float32)
    values = keep * jax.random.uniform(key_size, shape, jnp.float32, 0.25, 1.0)
    return values.astype(jnp.bfloat16)


def draw_tile_count(key, part):
    key = jax.random.fold_in(key, 23)
    key_base, key_full, key_level = jax.random.split(key, 3)
    devices = N_ROW * N_REP
    base = jax.random.randint(key_base, (devices, N_ROW), 1, SLOTS + 1)
    level = jax.random.randint(key_level, (devices, 1), 2, SLOTS + 1)
    base = jnp.minimum(base, level)
    full_block = jax.random.randint(key_full, (devices, 1), 0, N_ROW)
    blocks = jax.lax.broadcasted_iota(jnp.int32, (devices, N_ROW), 1)
    return jnp.where(blocks == full_block, SLOTS, base).astype(jnp.int32)


def plant(entries, stream_key, smallest, largest):
    extent = entries.shape
    place = [jax.random.randint(jax.random.fold_in(stream_key, axis), (), 0, extent[axis]) for axis in range(len(extent))]
    entries = entries.at[tuple(place)].set(smallest)
    longest = extent.index(max(extent))
    place[longest] = (place[longest] + 1) % extent[longest]
    return entries.at[tuple(place)].set(largest)


def steps_of(own_key, dims, cuts, least, largest):
    def one(axis_at, blocks):
        steps = jax.random.uniform(jax.random.fold_in(jax.random.fold_in(own_key, 6), axis_at), (blocks,), jnp.float32, least / len(cuts), largest / len(cuts))
        return jnp.repeat(jnp.exp(steps), dims[axis_at] // blocks).reshape((-1,) + (1,) * (len(dims) - axis_at - 1))

    gain = one(*cuts[0])
    for cut in cuts[1:]:
        gain = gain * one(*cut)
    return gain


def gaussian(stream_key, extent, spread, bound, shards=(), held_as=jnp.bfloat16):
    values = jax.random.normal(stream_key, extent, jnp.float32) * spread
    if len(shards) > 0:
        values = steps_of(stream_key, extent, shards, -0.22, 0.18) * values
    return jnp.clip(values, min=-bound, max=bound).astype(held_as)


def setup_inputs(seed: int = 0) -> dict:
    key_of = jax.random.split(jax.random.key(seed), 9)
    return {
        "features": gaussian(key_of[0], (NODES, F_IN), 1.0, 6.0, ((0, 256),)),
        "tile_values": draw_tile_values(jax.random.fold_in(key_of[8], 71), 0),
        "tile_rows": plant(jax.random.randint(key_of[2], (N_ROW * N_REP, N_ROW * SLOTS), 0, NODE_DEV // TILE), jax.random.fold_in(key_of[2], 1), 0, (NODE_DEV // TILE) - 1).astype(jnp.int32),
        "tile_cols": plant(jax.random.randint(key_of[3], (N_ROW * N_REP, N_ROW * SLOTS), 0, NODE_SUB // TILE), jax.random.fold_in(key_of[3], 1), 0, (NODE_SUB // TILE) - 1).astype(jnp.int32),
        "tile_count": draw_tile_count(jax.random.fold_in(key_of[8], 71), 0),
        "weight": gaussian(key_of[5], (F_IN, HID), 1.0, 6.0),
        "bias": gaussian(key_of[6], (HID,), 0.5, 3.0, (), jnp.float32),
        "cotangent": gaussian(key_of[7], (NODES, HID), 1.0, 6.0, ((0, 256),)),
    }


def activate(pre_values, upstream):
    output, pullback = jax.vjp(lambda v: jax.nn.gelu(v, approximate=True), pre_values)
    slope, = pullback(upstream.astype(pre_values.dtype))
    return (output, slope)

def reference(features, tile_values, tile_rows, tile_cols, tile_count, weight, bias, cotangent):
    devices = N_ROW * N_REP
    per_device = N_ROW * SLOTS
    row_tiles = NODE_DEV // TILE
    col_tiles = NODE_SUB // TILE
    tiles = tile_values.reshape(devices, per_device, TILE, TILE)
    slot_order = jnp.arange(per_device, dtype=jnp.int32)
    slot_block = slot_order // SLOTS
    live = ((slot_order % SLOTS)[None, :] < jnp.repeat(tile_count, SLOTS, axis=1)).astype(jnp.float32)
    tile_index = jnp.arange(row_tiles, dtype=jnp.int32)
    row_hot = (tile_rows[:, :, None] == tile_index[None, None, :]).astype(jnp.float32) * live[:, :, None]

    def row_weight(operands):
        tile_set, hot = operands
        sums = lax.optimization_barrier(jnp.sum(tile_set.astype(jnp.float32), axis=2))
        return jnp.einsum('sr,sk->rk', hot, sums).reshape(NODE_DEV)
    partial_degree = lax.map(row_weight, (tiles, row_hot))
    degree = 1.0 + lax.optimization_barrier(jnp.sum(partial_degree.reshape(N_ROW, N_REP, NODE_DEV), axis=1))
    scale = lax.rsqrt(degree).reshape(NODES)
    scaled = (scale[:, None] * features.astype(jnp.float32)).astype(jnp.bfloat16)
    sources = scaled.reshape(N_ROW, N_REP, col_tiles, TILE, F_IN)
    device_ids = jnp.arange(devices, dtype=jnp.int32)

    def forward_block(operands):
        tile_set, hot, columns, device = operands
        replica = device % N_REP
        source_set = jnp.take(sources, replica, axis=1)
        picked = source_set[slot_block, columns].astype(jnp.float32)
        products = jnp.einsum('skt,stf->skf', tile_set.astype(jnp.float32), picked)
        return jnp.einsum('sr,skf->rkf', hot, products).reshape(NODE_DEV, F_IN)
    partial_sums = lax.map(forward_block, (tiles, row_hot, tile_cols, device_ids))
    neighbours = lax.optimization_barrier(jnp.sum(partial_sums.reshape(N_ROW, N_REP, NODE_DEV, F_IN), axis=1)).reshape(NODES, F_IN)
    aggregated = scale[:, None] * (neighbours + scaled.astype(jnp.float32))
    agg_b = aggregated.astype(jnp.bfloat16)
    pre = jnp.dot(agg_b, weight, preferred_element_type=jnp.float32) + bias
    output, slope = activate(pre, cotangent)
    hidden_out = output.astype(jnp.bfloat16)
    dpre = slope.astype(jnp.bfloat16)
    grad_weight = lax.dot_general(agg_b, dpre, (((0,), (0,)), ((), ())), preferred_element_type=jnp.float32)
    back = (scale[:, None] * jnp.dot(dpre, weight.T, preferred_element_type=jnp.float32)).astype(jnp.bfloat16)
    back_blocks = back.reshape(N_ROW, row_tiles, TILE, F_IN)

    def backward_block(total, operands):
        tile_set, live_row, rows_of, columns, device = operands
        row_block = device // N_REP
        replica = device % N_REP
        own_rows = jnp.take(back_blocks, row_block, axis=0)
        picked = own_rows[rows_of].astype(jnp.float32) * live_row[:, None, None]
        products = jnp.einsum('skt,skf->stf', tile_set.astype(jnp.float32), picked)
        target = jnp.zeros((N_ROW, col_tiles, TILE, F_IN), jnp.float32).at[slot_block, columns].add(products)
        return (total.at[:, replica].add(target), None)
    start_total = jnp.zeros((N_ROW, N_REP, col_tiles, TILE, F_IN), jnp.float32)
    transposed, unused = lax.scan(backward_block, start_total, (tiles, live, tile_rows, tile_cols, device_ids))
    grad_features = (scale[:, None] * (transposed.reshape(NODES, F_IN) + back.astype(jnp.float32))).astype(jnp.bfloat16)
    return (hidden_out, grad_features, grad_weight)
```

```python
import functools

import jax
import jax.numpy as jnp
from jax import lax
from jax.experimental import pallas as pl
from jax.experimental.pallas import tpu as pltpu
from jax.sharding import Mesh, PartitionSpec as P

TILE = 128
SLOTS = 8
BF16 = jnp.bfloat16
F32 = jnp.float32
VMEM_BYTES = 48 * 1024 * 1024


def params():
    return pltpu.CompilerParams(
        dimension_semantics=("arbitrary",), vmem_limit_bytes=VMEM_BYTES
    )


def vmem():
    return pl.BlockSpec(memory_space=pltpu.VMEM)


def degree_kernel(group, row_tiles, rows, count, tiles, out, acc):
    step = pl.program_id(0)

    @pl.when(step == 0)
    def _():
        acc[...] = jnp.zeros_like(acc)

    ones = jnp.ones((16, TILE), BF16)
    for b in range(group):
        block = step * group + b
        live = count[0, block]
        stack = tiles[b * SLOTS : (b + 1) * SLOTS].reshape(SLOTS * TILE, TILE)
        sums = lax.dot_general(
            ones, stack, (((1,), (1,)), ((), ())), preferred_element_type=F32
        )
        for s in range(SLOTS):
            row = jnp.where(s < live, rows[0, block * SLOTS + s], row_tiles)
            acc[row] += sums[:8, s * TILE : (s + 1) * TILE]

    @pl.when(step == pl.num_programs(0) - 1)
    def _():
        for r in range(row_tiles):
            out[r : r + 1, :] = acc[r, 0:1, :]


def degree_call(tile_rows, tile_count, tile_values, row_tiles, group=4):
    slots = tile_values.shape[0]
    steps = slots // (SLOTS * group)
    return pl.pallas_call(
        functools.partial(degree_kernel, group, row_tiles),
        grid_spec=pltpu.PrefetchScalarGridSpec(
            num_scalar_prefetch=2,
            grid=(steps,),
            in_specs=[pl.BlockSpec((SLOTS * group, TILE, TILE), lambda i, *_: (i, 0, 0))],
            out_specs=pl.BlockSpec((row_tiles, TILE), lambda i, *_: (0, 0)),
            scratch_shapes=[pltpu.VMEM((row_tiles + 1, 8, TILE), F32)],
        ),
        out_shape=jax.ShapeDtypeStruct((row_tiles, TILE), F32),
        compiler_params=params(),
        name="degree",
    )(tile_rows, tile_count, tile_values)


def scale_kernel(copies, parts, features, row_out, col_out, spread):
    degree = 1.0 + jnp.sum(parts[...], axis=0)
    scale = lax.rsqrt(degree)
    row_out[...] = scale
    for c in range(scale.shape[0]):
        here = slice(c * TILE, (c + 1) * TILE)
        column = jnp.broadcast_to(scale[c : c + 1, :], (TILE, TILE)).T
        col_out[here, :] = column
        scaled = (column * features[here, :].astype(F32)).astype(BF16)
        for k in range(copies):
            spread[k, here, :] = scaled


def scale_call(parts, features, copies):
    sub, width = features.shape
    return pl.pallas_call(
        functools.partial(scale_kernel, copies),
        in_specs=[vmem(), vmem()],
        out_specs=(vmem(), vmem(), vmem()),
        out_shape=(
            jax.ShapeDtypeStruct((sub // TILE, TILE), F32),
            jax.ShapeDtypeStruct((sub, width), F32),
            jax.ShapeDtypeStruct((copies, sub, width), BF16),
        ),
        compiler_params=pltpu.CompilerParams(vmem_limit_bytes=VMEM_BYTES),
        name="scale",
    )(parts, features)


def forward_kernel(group, core, rows, cols, count, tiles, near, far, out, acc):
    step = pl.program_id(0)
    mine = core[0]

    @pl.when(step == 0)
    def _():
        acc[...] = jnp.zeros_like(acc)

    for b in range(group):
        for half, source in enumerate((near, far)):
            which = mine if half == 0 else 1 - mine
            first = b * 2 * SLOTS + which * SLOTS
            block = (step * group + b) * 2 + which
            live = count[0, block]
            stack = tiles[pl.ds(first, SLOTS)]
            pieces = []
            for s in range(SLOTS):
                column = cols[0, block * SLOTS + s]
                used = s < live
                tile = stack[s]
                blank = jnp.zeros_like(tile)
                left = jnp.where(used & (column == 0), tile, blank)
                right = jnp.where(used & (column != 0), tile, blank)
                pieces.append(jnp.concatenate([left, right], axis=1))
            products = jnp.dot(
                jnp.concatenate(pieces, axis=0), source[b], preferred_element_type=F32
            )
            for s in range(SLOTS):
                acc[rows[0, block * SLOTS + s]] += products[s * TILE : (s + 1) * TILE]

    @pl.when(step == pl.num_programs(0) - 1)
    def _():
        out[...] = acc[...].astype(BF16)


def forward_call(core, tile_rows, tile_cols, tile_count, tile_values, near, far, row_tiles, group=2):
    slots = tile_values.shape[0]
    steps = slots // (2 * SLOTS * group)
    sub, width = near.shape[1:]
    return pl.pallas_call(
        functools.partial(forward_kernel, group),
        grid_spec=pltpu.PrefetchScalarGridSpec(
            num_scalar_prefetch=4,
            grid=(steps,),
            in_specs=[
                pl.BlockSpec((2 * SLOTS * group, TILE, TILE), lambda i, *_: (i, 0, 0)),
                pl.BlockSpec((group, sub, width), lambda i, *_: (i, 0, 0)),
                pl.BlockSpec((group, sub, width), lambda i, *_: (i, 0, 0)),
            ],
            out_specs=pl.BlockSpec((row_tiles, TILE, width), lambda i, *_: (0, 0, 0)),
            scratch_shapes=[pltpu.VMEM((row_tiles, TILE, width), F32)],
        ),
        out_shape=jax.ShapeDtypeStruct((row_tiles, TILE, width), BF16),
        compiler_params=params(),
        name="forward",
    )(core, tile_rows, tile_cols, tile_count, tile_values, near, far)


def dense_kernel(parts, features, scale_col, scale_row, weight, bias, cotangent, hidden, back_own, pay):
    sub = features.shape[0]
    replicas = parts.shape[0]
    column = scale_col[...]
    total = (column * features[...].astype(F32)).astype(BF16).astype(F32)
    for r in range(replicas):
        total += parts[r].astype(F32)
    agg_b = (column * total).astype(BF16)
    w = weight[...]
    v = jnp.dot(agg_b, w, preferred_element_type=F32) + bias[...]
    root = 0.7978845608028654
    square = v * v
    t = jnp.tanh(root * (v + 0.044715 * (square * v)))
    cdf = 0.5 * (1.0 + t)
    hidden[...] = (v * cdf).astype(BF16)
    slope = cdf + 0.5 * v * ((1.0 - t) * (1.0 + t)) * (root * (1.0 + (3 * 0.044715) * square))
    dpre = (cotangent[...].astype(F32) * slope).astype(BF16)
    grad = lax.dot_general(agg_b, dpre, (((0,), (0,)), ((), ())), preferred_element_type=F32)
    back = lax.dot_general(w, dpre, (((1,), (1,)), ((), ())), preferred_element_type=F32)
    for c in range(sub // TILE):
        here = slice(c * TILE, (c + 1) * TILE)
        piece = (back[:, here] * scale_row[c : c + 1, :]).astype(BF16)
        back_own[here, :] = piece
        for r in range(replicas):
            pay[r, here, :] = piece
    grad_b = grad.astype(BF16)
    rows = grad.shape[0] // replicas
    for r in range(replicas):
        for h in range(grad.shape[1] // TILE):
            pay[r, sub + h * rows : sub + (h + 1) * rows, :] = grad_b[
                r * rows : (r + 1) * rows, h * TILE : (h + 1) * TILE
            ]


def dense_call(parts, features, scale_col, scale_row, weight, bias, cotangent):
    sub, width = features.shape
    replicas = parts.shape[0]
    hid = weight.shape[1]
    extra = width // replicas * (hid // TILE)
    return pl.pallas_call(
        dense_kernel,
        in_specs=[vmem()] * 7,
        out_specs=(vmem(), vmem(), vmem()),
        out_shape=(
            jax.ShapeDtypeStruct((sub, hid), BF16),
            jax.ShapeDtypeStruct((sub, width), BF16),
            jax.ShapeDtypeStruct((replicas, sub + extra, width), BF16),
        ),
        compiler_params=pltpu.CompilerParams(vmem_limit_bytes=VMEM_BYTES),
        name="dense",
    )(parts, features, scale_col, scale_row, weight, bias, cotangent)


def backward_kernel(group, core, rows, cols, count, tiles, back, near, far, grad):
    step = pl.program_id(0)
    mine = core[0]
    sub = 2 * TILE
    replicas, height, width = back.shape

    @pl.when(step == 0)
    def _():
        grad[...] = jnp.sum(back[:, sub:, :].astype(F32), axis=0).astype(BF16)

    for b in range(group):
        for half, target in enumerate((near, far)):
            which = mine if half == 0 else 1 - mine
            first = b * 2 * SLOTS + which * SLOTS
            block = (step * group + b) * 2 + which
            live = count[0, block]
            pieces = []
            for s in range(SLOTS):
                column = cols[0, block * SLOTS + s]
                row = rows[0, block * SLOTS + s]
                used = s < live
                tile = back[row // 2, pl.ds(pl.multiple_of((row % 2) * TILE, TILE), TILE), :]
                blank = jnp.zeros_like(tile)
                top = jnp.where(used & (column == 0), tile, blank)
                low = jnp.where(used & (column != 0), tile, blank)
                pieces.append(jnp.concatenate([top, low], axis=0))
            stack = tiles[pl.ds(first, SLOTS)].reshape(SLOTS * TILE, TILE)
            products = jnp.dot(
                jnp.concatenate(pieces, axis=1), stack, preferred_element_type=F32
            )
            target[b, :sub, :] = products.astype(BF16)
            target[b, sub:, :] = grad[...]


def backward_call(core, tile_rows, tile_cols, tile_count, tile_values, back, group=2):
    slots = tile_values.shape[0]
    steps = slots // (2 * SLOTS * group)
    replicas, height, width = back.shape
    out = pl.BlockSpec((group, height, width), lambda i, *_: (i, 0, 0))
    shape = jax.ShapeDtypeStruct((steps * group, height, width), BF16)
    return pl.pallas_call(
        functools.partial(backward_kernel, group),
        grid_spec=pltpu.PrefetchScalarGridSpec(
            num_scalar_prefetch=4,
            grid=(steps,),
            in_specs=[
                pl.BlockSpec((2 * SLOTS * group, TILE, TILE), lambda i, *_: (i, 0, 0)),
                pl.BlockSpec((replicas, height, width), lambda i, *_: (0, 0, 0)),
            ],
            out_specs=(out, out),
            scratch_shapes=[pltpu.VMEM((height - 2 * TILE, width), BF16)],
        ),
        out_shape=(shape, shape),
        compiler_params=params(),
        name="backward",
    )(core, tile_rows, tile_cols, tile_count, tile_values, back)


def final_kernel(parts, back_own, scale_row, grad_features, grad_piece):
    sub = back_own.shape[0]
    total = jnp.sum(parts[...].astype(F32), axis=0)
    for c in range(sub // TILE):
        here = slice(c * TILE, (c + 1) * TILE)
        value = (total[here, :] + back_own[here, :].astype(F32)) * scale_row[c : c + 1, :]
        grad_features[here, :] = value.T.astype(BF16)
    for r in range(grad_piece.shape[0]):
        grad_piece[r] = total[sub:, :]


def final_call(parts, back_own, scale_row, replicas):
    sub, width = back_own.shape
    extra = parts.shape[1] - sub
    return pl.pallas_call(
        final_kernel,
        in_specs=[vmem()] * 3,
        out_specs=(vmem(), vmem()),
        out_shape=(
            jax.ShapeDtypeStruct((sub, width), BF16),
            jax.ShapeDtypeStruct((replicas, extra, width), F32),
        ),
        compiler_params=pltpu.CompilerParams(vmem_limit_bytes=VMEM_BYTES),
        name="final",
    )(parts, back_own, scale_row)


SWAP = ((0, 1), (1, 0))


def body(features, tile_values, tile_rows, tile_cols, tile_count, weight, bias, cotangent):
    replicas = lax.axis_size("rep")
    sub, width = features.shape
    row_tiles = sub * replicas // TILE
    ring = lax.axis_size("zed") * lax.axis_size("pair")
    core = lax.axis_index("core").astype(jnp.int32).reshape(1)

    partial = degree_call(tile_rows, tile_count, tile_values, row_tiles)
    parts = lax.all_to_all(
        partial.reshape(replicas, sub // TILE, TILE), "rep", 0, 0, tiled=True
    )
    scale_row, scale_col, spread = scale_call(parts, features, ring)
    near = lax.all_to_all(spread, ("zed", "pair"), 0, 0, tiled=True)
    far = lax.ppermute(near, "core", SWAP)
    sums = forward_call(
        core, tile_rows, tile_cols, tile_count, tile_values, near, far, row_tiles
    )
    sums = lax.all_to_all(sums.reshape(replicas, sub, width), "rep", 0, 0, tiled=True)
    hidden, back_own, pay = dense_call(
        sums, features, scale_col, scale_row, weight, bias.reshape(1, -1), cotangent
    )
    back = lax.all_to_all(pay, "rep", 0, 0, tiled=True)
    near, far = backward_call(core, tile_rows, tile_cols, tile_count, tile_values, back)
    near = near + lax.ppermute(far, "core", SWAP)
    near = lax.all_to_all(near, ("zed", "pair"), 0, 0, tiled=True)
    grad_features, piece = final_call(near, back_own, scale_row, replicas)
    piece = lax.all_to_all(piece, "rep", 0, 0, tiled=True)
    hid = weight.shape[1]
    rows = width // replicas
    grad_weight = (
        piece.reshape(replicas, hid // TILE, rows, TILE)
        .transpose(0, 2, 1, 3)
        .reshape(width, hid)
    )
    return hidden, grad_features, grad_weight


def solution(mesh):
    rows, replicas = mesh.devices.shape
    fine = Mesh(
        mesh.devices.reshape(rows // 4, 2, 2, replicas), ("zed", "pair", "core", "rep")
    )
    whole = ("zed", "pair", "core", "rep")
    placed = (
        P(whole, None),
        P(whole, None, None),
        P(whole, None),
        P(whole, None),
        P(whole, None),
        P(),
        P(),
        P(whole, None),
    )
    return jax.shard_map(
        body,
        mesh=fine,
        in_specs=placed,
        out_specs=(P(whole, None), P(whole, None), P()),
        check_vma=False,
    )
```

```python
import functools

import jax
import jax.numpy as jnp
from jax import lax
from jax.experimental import pallas as pl
from jax.experimental.pallas import tpu as pltpu
from jax.sharding import Mesh, PartitionSpec as P

TILE = 128
SLOTS = 8
BF16 = jnp.bfloat16
F32 = jnp.float32
VMEM_BYTES = 16 * 1024 * 1024
DEGREE_BYTES = 50 * 1024 * 1024
REACH = 4


def params():
    return pltpu.CompilerParams(vmem_limit_bytes=VMEM_BYTES)


def vmem():
    return pl.BlockSpec(memory_space=pltpu.VMEM)


def smem():
    return pl.BlockSpec(memory_space=pltpu.SMEM)


def lookup(meta):
    slots = (meta.shape[1] - 3) * SLOTS // (2 * SLOTS + 1)
    blocks = slots // SLOTS

    def rows(slot):
        return meta[0, slot]

    def cols(slot):
        return meta[0, slots + slot]

    def count(block):
        return meta[0, 2 * slots + block]

    def place(axis):
        return meta[0, 2 * slots + blocks + axis]

    return rows, cols, count, place


def degree_kernel(chunks, meta, tiles, out, held, acc, sems):
    rows, _, count, _ = lookup(meta)
    row_tiles = out.shape[0]
    size = tiles.shape[0] // chunks
    copies = [
        pltpu.make_async_copy(
            tiles.at[pl.ds(c * size, size)], held.at[pl.ds(c * size, size)], sems.at[c]
        )
        for c in range(chunks)
    ]
    for copy in copies:
        copy.start()
    acc[...] = jnp.zeros_like(acc)
    ones = jnp.ones((16, TILE), BF16)
    for c in range(chunks):
        copies[c].wait()
        for block in range(c * size // SLOTS, (c + 1) * size // SLOTS):
            live = count(block)
            stack = held[block * SLOTS : (block + 1) * SLOTS].reshape(SLOTS * TILE, TILE)
            sums = lax.dot_general(
                ones, stack, (((1,), (1,)), ((), ())), preferred_element_type=F32
            )
            for s in range(SLOTS):
                row = jnp.where(s < live, rows(block * SLOTS + s), row_tiles)
                acc[row] += sums[:8, s * TILE : (s + 1) * TILE]
    for r in range(row_tiles):
        out[r : r + 1, :] = acc[r, 0:1, :]


def degree_call(meta, tiles, row_tiles, chunks=4):
    return pl.pallas_call(
        functools.partial(degree_kernel, chunks),
        in_specs=[smem(), pl.BlockSpec(memory_space=pl.ANY)],
        out_specs=vmem(),
        out_shape=jax.ShapeDtypeStruct((row_tiles, TILE), F32),
        scratch_shapes=[
            pltpu.VMEM(tiles.shape, BF16),
            pltpu.VMEM((row_tiles + 1, 8, TILE), F32),
            pltpu.SemaphoreType.DMA((chunks,)),
        ],
        compiler_params=pltpu.CompilerParams(vmem_limit_bytes=DEGREE_BYTES),
        name="degree",
    )(meta, tiles)


def join_kernel(one, two, three, four, out, half):
    for i, piece in enumerate((one, two, three, four)):
        out[i] = piece[...]
        if i < 2:
            half[i] = piece[...]


def join_call(*pieces):
    shape = pieces[0].shape
    return pl.pallas_call(
        join_kernel,
        in_specs=[vmem()] * 4,
        out_specs=(vmem(), vmem()),
        out_shape=(
            jax.ShapeDtypeStruct((4,) + shape, BF16),
            jax.ShapeDtypeStruct((2,) + shape, BF16),
        ),
        compiler_params=params(),
        name="join",
    )(*pieces)


def scale_kernel(parts, row_out, col_out, spread):
    degree = 1.0 + jnp.sum(parts[...], axis=0)
    scale = lax.rsqrt(degree)
    row_out[...] = scale
    for c in range(scale.shape[0]):
        here = slice(c * TILE, (c + 1) * TILE)
        col_out[here, :] = jnp.broadcast_to(scale[c : c + 1, :], (TILE, TILE)).T
    spread[...] = jnp.broadcast_to(scale[None], spread.shape)


def scale_call(parts, copies):
    halves = parts.shape[1]
    return pl.pallas_call(
        scale_kernel,
        in_specs=[vmem()],
        out_specs=(vmem(), vmem(), vmem()),
        out_shape=(
            jax.ShapeDtypeStruct((halves, TILE), F32),
            jax.ShapeDtypeStruct((halves * TILE, TILE), F32),
            jax.ShapeDtypeStruct((copies, halves, TILE), F32),
        ),
        compiler_params=params(),
        name="scale",
    )(parts)


def block_of(place, core, length, ahead, a, b):
    there = lax.rem(place(0) + ahead + length, length)
    return there * 4 + (place(1) ^ a) * 2 + (core ^ b)


def forward_kernel(length, first, meta, tiles, scales, *refs):
    rows, cols, count, place = lookup(meta)
    core = place(2)
    sign = 1 - 2 * core
    if first:
        sources, (out, scaled) = refs[:-2], refs[-2:]
        acc = out
        work = [(sources[0], i, core, 0) for i in range(4)]
        for k in range(1, REACH + 1):
            work += [(sources[k], i, core, -sign * k) for i in range(sources[k].shape[0])]
    else:
        before, sources, (out, scaled, acc) = refs[0], refs[1:-3], refs[-3:]
        work = []
        for k in range(1, REACH + 1):
            piece = sources[k - 1]
            work += [(piece, i, 1 - core, sign * k) for i in range(piece.shape[0])]
    row_tiles = acc.shape[0] - 1
    acc[...] = jnp.zeros_like(acc)
    for n, (source, i, side, ahead) in enumerate(work):
        block = block_of(place, side, length, ahead, i % 2, i // 2)
        live = count(block)
        for c in range(2):
            column = jnp.broadcast_to(scales[block, c : c + 1, :], (TILE, TILE)).T
            plain = source[i, c * TILE : (c + 1) * TILE, :].astype(F32)
            scaled[n, c] = (column * plain).astype(BF16)
        for s in range(SLOTS):
            slot = block * SLOTS + s
            product = jnp.dot(
                tiles[slot], scaled[n, cols(slot)], preferred_element_type=F32
            )
            row = jnp.where(s < live, rows(slot), row_tiles)
            acc[row] += product
    if not first:
        out[...] = (before[:row_tiles] + acc[:row_tiles]).astype(BF16)


def forward_call(length, meta, tiles, scales, before, sources, row_tiles):
    blocks = scales.shape[0]
    width = sources[0].shape[2]
    first = before is None
    total = (row_tiles + 1, TILE, width)
    given = list(sources) if first else [before, *sources]
    scratch = [pltpu.VMEM((blocks, 2, TILE, width), BF16)]
    if first:
        shape = jax.ShapeDtypeStruct(total, F32)
    else:
        shape = jax.ShapeDtypeStruct((row_tiles, TILE, width), BF16)
        scratch.append(pltpu.VMEM(total, F32))
    return pl.pallas_call(
        functools.partial(forward_kernel, length, first),
        in_specs=[smem()] + [vmem()] * (2 + len(given)),
        out_specs=vmem(),
        out_shape=shape,
        scratch_shapes=scratch,
        compiler_params=params(),
        name="forward_near" if first else "forward_far",
    )(meta, tiles, scales, *given)


def dense_kernel(parts, features, scale_col, scale_row, weight, bias, cotangent, hidden, back_own, pay):
    sub = features.shape[0]
    replicas = parts.shape[0]
    column = scale_col[...]
    total = (column * features[...].astype(F32)).astype(BF16).astype(F32)
    for r in range(replicas):
        total += parts[r].astype(F32)
    agg_b = (column * total).astype(BF16)
    w = weight[...]
    v = jnp.dot(agg_b, w, preferred_element_type=F32) + bias[...]
    root = 0.7978845608028654
    square = v * v
    t = jnp.tanh(root * (v + 0.044715 * (square * v)))
    cdf = 0.5 * (1.0 + t)
    hidden[...] = (v * cdf).astype(BF16)
    slope = cdf + 0.5 * v * ((1.0 - t) * (1.0 + t)) * (root * (1.0 + (3 * 0.044715) * square))
    dpre = (cotangent[...].astype(F32) * slope).astype(BF16)
    grad = lax.dot_general(agg_b, dpre, (((0,), (0,)), ((), ())), preferred_element_type=F32)
    back = lax.dot_general(w, dpre, (((1,), (1,)), ((), ())), preferred_element_type=F32)
    for c in range(sub // TILE):
        here = slice(c * TILE, (c + 1) * TILE)
        piece = (back[:, here] * scale_row[c : c + 1, :]).astype(BF16)
        back_own[here, :] = piece
        for r in range(replicas):
            pay[r, here, :] = piece
    grad_b = grad.astype(BF16)
    rows = grad.shape[0] // replicas
    for r in range(replicas):
        for h in range(grad.shape[1] // TILE):
            pay[r, sub + h * rows : sub + (h + 1) * rows, :] = grad_b[
                r * rows : (r + 1) * rows, h * TILE : (h + 1) * TILE
            ]


def dense_call(parts, features, scale_col, scale_row, weight, bias, cotangent):
    sub, width = features.shape
    replicas = parts.shape[0]
    hid = weight.shape[1]
    extra = width // replicas * (hid // TILE)
    return pl.pallas_call(
        dense_kernel,
        in_specs=[vmem()] * 7,
        out_specs=(vmem(), vmem(), vmem()),
        out_shape=(
            jax.ShapeDtypeStruct((sub, hid), BF16),
            jax.ShapeDtypeStruct((sub, width), BF16),
            jax.ShapeDtypeStruct((replicas, sub + extra, width), BF16),
        ),
        compiler_params=params(),
        name="dense",
    )(parts, features, scale_col, scale_row, weight, bias, cotangent)


def backward_kernel(length, mine, meta, tiles, back, *outs):
    rows, cols, count, place = lookup(meta)
    side = place(2) if mine else 1 - place(2)
    sign = 1 - 2 * side
    for a in (1, 0):
        work = [(sign * k, b) for k in range(1, REACH) for b in range(2)]
        work += [(REACH, 0), (0, 0)]
        for n, (ahead, b) in enumerate(work):
            block = block_of(place, side, length, ahead, a, b)
            live = count(block)
            low = jnp.zeros((TILE, TILE), F32)
            high = low
            for s in range(SLOTS):
                slot = block * SLOTS + s
                row = rows(slot)
                column = cols(slot)
                used = s < live
                tile = back[row // 2, pl.ds(pl.multiple_of((row % 2) * TILE, TILE), TILE), :]
                product = jnp.dot(tile, tiles[slot], preferred_element_type=F32)
                low += jnp.where(used & (column == 0), product, 0.0)
                high += jnp.where(used & (column != 0), product, 0.0)
            outs[a][n, :TILE] = low.astype(BF16)
            outs[a][n, TILE:] = high.astype(BF16)
    if len(outs) == 3:
        piece = jnp.sum(back[:, 2 * TILE :, :].astype(F32), axis=0).astype(BF16)
        for r in range(outs[2].shape[0]):
            outs[2][r] = piece


def backward_call(length, mine, meta, tiles, back):
    height, width = back.shape[1:]
    blocks = tiles.shape[0] // SLOTS
    shapes = [jax.ShapeDtypeStruct((length, 2 * TILE, width), BF16)] * 2
    if mine:
        shapes.append(jax.ShapeDtypeStruct((blocks, height - 2 * TILE, width), BF16))
    return pl.pallas_call(
        functools.partial(backward_kernel, length, mine),
        in_specs=[smem()] + [vmem()] * 2,
        out_specs=(vmem(),) * len(shapes),
        out_shape=tuple(shapes),
        compiler_params=params(),
        name="backward_near" if mine else "backward_far",
    )(meta, tiles, back)


def grad_kernel(parts, out):
    out[...] = jnp.broadcast_to(jnp.sum(parts[...].astype(F32), axis=0)[None], out.shape)


def grad_call(parts, replicas):
    return pl.pallas_call(
        grad_kernel,
        in_specs=[vmem()],
        out_specs=vmem(),
        out_shape=jax.ShapeDtypeStruct((replicas,) + parts.shape[1:], F32),
        compiler_params=params(),
        name="grad",
    )(parts)


def fold_kernel(one, two, three, four, own, keep, give):
    total = one[...].astype(F32) + two[...].astype(F32) + three[...].astype(F32)
    keep[...] = total[0] + four[0].astype(F32) + own[0].astype(F32)
    give[...] = total[1].astype(BF16)


def fold_call(parts, own):
    shape = own.shape[1:]
    return pl.pallas_call(
        fold_kernel,
        in_specs=[vmem()] * 5,
        out_specs=(vmem(), vmem()),
        out_shape=(jax.ShapeDtypeStruct(shape, F32), jax.ShapeDtypeStruct(shape, BF16)),
        compiler_params=params(),
        name="fold",
    )(*parts, own)


def final_kernel(keep, got, back_own, scale_row, pieces, grad_features, grad_weight):
    for c in range(back_own.shape[0] // TILE):
        here = slice(c * TILE, (c + 1) * TILE)
        value = keep[here, :] + got[here, :].astype(F32) + back_own[here, :].astype(F32)
        grad_features[here, :] = (value * scale_row[c : c + 1, :]).T.astype(BF16)
    replicas, height, width = pieces.shape
    halves = grad_weight.shape[1] // width
    rows = height // halves
    for r in range(replicas):
        for h in range(halves):
            grad_weight[r * rows : (r + 1) * rows, h * width : (h + 1) * width] = pieces[
                r, h * rows : (h + 1) * rows, :
            ]


def final_call(keep, got, back_own, scale_row, pieces):
    replicas, height, width = pieces.shape
    return pl.pallas_call(
        final_kernel,
        in_specs=[vmem()] * 5,
        out_specs=(vmem(), vmem()),
        out_shape=(
            jax.ShapeDtypeStruct(back_own.shape, BF16),
            jax.ShapeDtypeStruct((TILE, replicas * height * width // TILE), F32),
        ),
        compiler_params=params(),
        name="final",
    )(keep, got, back_own, scale_row, pieces)


SWAP = ((0, 1), (1, 0))


def body(features, tile_values, tile_rows, tile_cols, tile_count, weight, bias, cotangent):
    replicas = lax.axis_size("rep")
    length = lax.axis_size("zed")
    blocks = tile_count.shape[1]
    sub, width = features.shape
    row_tiles = sub * replicas // TILE
    place = [lax.axis_index(n).astype(jnp.int32).reshape(1, 1) for n in ("zed", "pair", "core")]
    meta = jnp.concatenate([tile_rows, tile_cols, tile_count, *place], axis=1)

    def along(value, k):
        moves = [
            (z * 2 + c, (z + (1 - 2 * c) * k) % length * 2 + c)
            for z in range(length)
            for c in range(2)
        ]
        return lax.ppermute(value, ("zed", "core"), moves)

    def swap(value, axis):
        return lax.ppermute(value, axis, SWAP)

    partner = swap(features, "pair")
    sibling = swap(features, "core")
    partial = degree_call(meta, tile_values, row_tiles)
    partner, partial = lax.optimization_barrier((partner, partial))
    own, two = join_call(features, partner, sibling, swap(partner, "core"))
    own, two, partial = lax.optimization_barrier((own, two, partial))
    near = [along(own if k < REACH else two, k) for k in range(1, REACH + 1)]
    parts = lax.all_to_all(
        partial.reshape(replicas, sub // TILE, TILE), "rep", 0, 0, tiled=True
    )
    scale_row, scale_col, spread = scale_call(parts, blocks)
    scales = lax.all_to_all(spread, ("zed", "pair", "core"), 0, 0, tiled=True)
    scales, near = lax.optimization_barrier((scales, near))
    far = [swap(value, "core") for value in near]
    sums = forward_call(length, meta, tile_values, scales, None, [own, *near], row_tiles)
    sums = forward_call(length, meta, tile_values, scales, sums, far, row_tiles)
    sums = lax.all_to_all(sums.reshape(replicas, sub, width), "rep", 0, 0, tiled=True)
    hidden, back_own, pay = dense_call(
        sums, features, scale_col, scale_row, weight, bias.reshape(1, -1), cotangent
    )
    back = lax.all_to_all(pay, "rep", 0, 0, tiled=True)

    far = backward_call(length, False, meta, tile_values, back)
    far = [swap(far[1], "core"), swap(far[0], "core")]
    *near, piece = backward_call(length, True, meta, tile_values, back)
    other = swap(near[1] + far[0], "pair")
    mine = near[0] + far[1]

    piece = lax.all_to_all(piece, ("zed", "pair", "core"), 0, 0, tiled=True)
    mine = mine + other
    parts = [
        along(mine[2 * k - 2 : 2 * k] if k < REACH else mine[2 * k - 2 : 2 * k - 1], k)
        for k in range(1, REACH + 1)
    ]
    piece = lax.all_to_all(grad_call(piece, replicas), "rep", 0, 0, tiled=True)
    keep, give = fold_call(parts, mine[2 * REACH - 1 :])
    grad_features, grad_weight = final_call(
        keep, swap(give, "core"), back_own, scale_row, piece
    )
    return hidden, grad_features, grad_weight


def solution(mesh):
    rows, replicas = mesh.devices.shape
    fine = Mesh(
        mesh.devices.reshape(rows // 4, 2, 2, replicas), ("zed", "pair", "core", "rep")
    )
    whole = ("zed", "pair", "core", "rep")
    placed = (
        P(whole, None),
        P(whole, None, None),
        P(whole, None),
        P(whole, None),
        P(whole, None),
        P(),
        P(),
        P(whole, None),
    )
    return jax.shard_map(
        body,
        mesh=fine,
        in_specs=placed,
        out_specs=(P(whole, None), P(whole, None), P()),
        check_vma=False,
    )
```

```python
import functools

import jax
import jax.numpy as jnp
from jax import lax
from jax.experimental import pallas as pl
from jax.experimental.pallas import tpu as pltpu
from jax.sharding import Mesh, PartitionSpec as P

TILE = 128
SLOTS = 8
BF16 = jnp.bfloat16
F32 = jnp.float32
VMEM_BYTES = 16 * 1024 * 1024
DEGREE_BYTES = 50 * 1024 * 1024
REACH = 4


def params():
    return pltpu.CompilerParams(vmem_limit_bytes=VMEM_BYTES)


def vmem():
    return pl.BlockSpec(memory_space=pltpu.VMEM)


def smem():
    return pl.BlockSpec(memory_space=pltpu.SMEM)


def lookup(meta):
    slots = (meta.shape[1] - 3) * SLOTS // (2 * SLOTS + 1)
    blocks = slots // SLOTS

    def rows(slot):
        return meta[0, slot]

    def cols(slot):
        return meta[0, slots + slot]

    def count(block):
        return meta[0, 2 * slots + block]

    def place(axis):
        return meta[0, 2 * slots + blocks + axis]

    return rows, cols, count, place


def degree_kernel(chunks, meta, tiles, out, held, acc, sems):
    rows, _, count, _ = lookup(meta)
    row_tiles = out.shape[0]
    size = tiles.shape[0] // chunks
    copies = [
        pltpu.make_async_copy(
            tiles.at[pl.ds(c * size, size)], held.at[pl.ds(c * size, size)], sems.at[c]
        )
        for c in range(chunks)
    ]
    for copy in copies:
        copy.start()
    acc[...] = jnp.zeros_like(acc)
    ones = jnp.ones((16, TILE), BF16)
    for c in range(chunks):
        copies[c].wait()
        for block in range(c * size // SLOTS, (c + 1) * size // SLOTS):
            live = count(block)
            stack = held[block * SLOTS : (block + 1) * SLOTS].reshape(SLOTS * TILE, TILE)
            sums = lax.dot_general(
                ones, stack, (((1,), (1,)), ((), ())), preferred_element_type=F32
            )
            for s in range(SLOTS):
                row = jnp.where(s < live, rows(block * SLOTS + s), row_tiles)
                acc[row] += sums[:8, s * TILE : (s + 1) * TILE]
    for r in range(row_tiles):
        out[r : r + 1, :] = acc[r, 0:1, :]


def degree_call(meta, tiles, row_tiles, chunks=4):
    return pl.pallas_call(
        functools.partial(degree_kernel, chunks),
        in_specs=[smem(), pl.BlockSpec(memory_space=pl.ANY)],
        out_specs=vmem(),
        out_shape=jax.ShapeDtypeStruct((row_tiles, TILE), F32),
        scratch_shapes=[
            pltpu.VMEM(tiles.shape, BF16),
            pltpu.VMEM((row_tiles + 1, 8, TILE), F32),
            pltpu.SemaphoreType.DMA((chunks,)),
        ],
        compiler_params=pltpu.CompilerParams(vmem_limit_bytes=DEGREE_BYTES),
        name="degree",
    )(meta, tiles)


def join_kernel(one, two, three, four, out, half):
    for i, piece in enumerate((one, two, three, four)):
        out[i] = piece[...]
        if i < 2:
            half[i] = piece[...]


def join_call(*pieces):
    shape = pieces[0].shape
    return pl.pallas_call(
        join_kernel,
        in_specs=[vmem()] * 4,
        out_specs=(vmem(), vmem()),
        out_shape=(
            jax.ShapeDtypeStruct((4,) + shape, BF16),
            jax.ShapeDtypeStruct((2,) + shape, BF16),
        ),
        compiler_params=params(),
        name="join",
    )(*pieces)


def scale_kernel(parts, row_out, col_out, spread):
    degree = 1.0 + jnp.sum(parts[...], axis=0)
    scale = lax.rsqrt(degree)
    row_out[...] = scale
    for c in range(scale.shape[0]):
        here = slice(c * TILE, (c + 1) * TILE)
        col_out[here, :] = jnp.broadcast_to(scale[c : c + 1, :], (TILE, TILE)).T
    spread[...] = jnp.broadcast_to(scale[None], spread.shape)


def scale_call(parts, copies):
    halves = parts.shape[1]
    return pl.pallas_call(
        scale_kernel,
        in_specs=[vmem()],
        out_specs=(vmem(), vmem(), vmem()),
        out_shape=(
            jax.ShapeDtypeStruct((halves, TILE), F32),
            jax.ShapeDtypeStruct((halves * TILE, TILE), F32),
            jax.ShapeDtypeStruct((copies, halves, TILE), F32),
        ),
        compiler_params=params(),
        name="scale",
    )(parts)


def block_of(place, core, length, ahead, a, b):
    there = lax.rem(place(0) + ahead + length, length)
    return there * 4 + (place(1) ^ a) * 2 + (core ^ b)


def forward_kernel(length, first, meta, tiles, scales, *refs):
    rows, cols, count, place = lookup(meta)
    core = place(2)
    sign = 1 - 2 * core
    if first:
        sources, (out, scaled) = refs[:-2], refs[-2:]
        acc = out
        work = [(sources[0], i, core, 0) for i in range(4)]
        for k in range(1, REACH + 1):
            work += [(sources[k], i, core, -sign * k) for i in range(sources[k].shape[0])]
    else:
        before, sources, (out, scaled, acc) = refs[0], refs[1:-3], refs[-3:]
        work = []
        for k in range(1, REACH + 1):
            piece = sources[k - 1]
            work += [(piece, i, 1 - core, sign * k) for i in range(piece.shape[0])]
    row_tiles = acc.shape[0] - 1
    acc[...] = jnp.zeros_like(acc)
    for n, (source, i, side, ahead) in enumerate(work):
        block = block_of(place, side, length, ahead, i % 2, i // 2)
        live = count(block)
        for c in range(2):
            column = jnp.broadcast_to(scales[block, c : c + 1, :], (TILE, TILE)).T
            plain = source[i, c * TILE : (c + 1) * TILE, :].astype(F32)
            scaled[n, c] = (column * plain).astype(BF16)
        for s in range(SLOTS):
            slot = block * SLOTS + s
            product = jnp.dot(
                tiles[slot], scaled[n, cols(slot)], preferred_element_type=F32
            )
            row = jnp.where(s < live, rows(slot), row_tiles)
            acc[row] += product
    if not first:
        out[...] = (before[:row_tiles] + acc[:row_tiles]).astype(BF16)


def forward_call(length, meta, tiles, scales, before, sources, row_tiles):
    blocks = scales.shape[0]
    width = sources[0].shape[2]
    first = before is None
    total = (row_tiles + 1, TILE, width)
    given = list(sources) if first else [before, *sources]
    scratch = [pltpu.VMEM((blocks, 2, TILE, width), BF16)]
    if first:
        shape = jax.ShapeDtypeStruct(total, F32)
    else:
        shape = jax.ShapeDtypeStruct((row_tiles, TILE, width), BF16)
        scratch.append(pltpu.VMEM(total, F32))
    return pl.pallas_call(
        functools.partial(forward_kernel, length, first),
        in_specs=[smem()] + [vmem()] * (2 + len(given)),
        out_specs=vmem(),
        out_shape=shape,
        scratch_shapes=scratch,
        compiler_params=params(),
        name="forward_near" if first else "forward_far",
    )(meta, tiles, scales, *given)


def dense_kernel(parts, features, scale_col, scale_row, weight, bias, cotangent, hidden, back_own, pay):
    sub = features.shape[0]
    replicas = parts.shape[0]
    column = scale_col[...]
    total = (column * features[...].astype(F32)).astype(BF16).astype(F32)
    for r in range(replicas):
        total += parts[r].astype(F32)
    agg_b = (column * total).astype(BF16)
    w = weight[...]
    v = jnp.dot(agg_b, w, preferred_element_type=F32) + bias[...]
    root = 0.7978845608028654
    square = v * v
    t = jnp.tanh(root * (v + 0.044715 * (square * v)))
    cdf = 0.5 * (1.0 + t)
    hidden[...] = (v * cdf).astype(BF16)
    slope = cdf + 0.5 * v * ((1.0 - t) * (1.0 + t)) * (root * (1.0 + (3 * 0.044715) * square))
    dpre = (cotangent[...].astype(F32) * slope).astype(BF16)
    grad = lax.dot_general(agg_b, dpre, (((0,), (0,)), ((), ())), preferred_element_type=F32)
    back = lax.dot_general(w, dpre, (((1,), (1,)), ((), ())), preferred_element_type=F32)
    for c in range(sub // TILE):
        here = slice(c * TILE, (c + 1) * TILE)
        piece = (back[:, here] * scale_row[c : c + 1, :]).astype(BF16)
        back_own[here, :] = piece
        for r in range(replicas):
            pay[r, here, :] = piece
    grad_b = grad.astype(BF16)
    rows = grad.shape[0] // replicas
    for r in range(replicas):
        for h in range(grad.shape[1] // TILE):
            pay[r, sub + h * rows : sub + (h + 1) * rows, :] = grad_b[
                r * rows : (r + 1) * rows, h * TILE : (h + 1) * TILE
            ]


def dense_call(parts, features, scale_col, scale_row, weight, bias, cotangent):
    sub, width = features.shape
    replicas = parts.shape[0]
    hid = weight.shape[1]
    extra = width // replicas * (hid // TILE)
    return pl.pallas_call(
        dense_kernel,
        in_specs=[vmem()] * 7,
        out_specs=(vmem(), vmem(), vmem()),
        out_shape=(
            jax.ShapeDtypeStruct((sub, hid), BF16),
            jax.ShapeDtypeStruct((sub, width), BF16),
            jax.ShapeDtypeStruct((replicas, sub + extra, width), BF16),
        ),
        compiler_params=params(),
        name="dense",
    )(parts, features, scale_col, scale_row, weight, bias, cotangent)


LONG = ((3, 0), (3, 1), (2, 0), (2, 1))
SHORT = ((1, 0), (1, 1), (4, 0), (0, 0))


def backward_kernel(length, mine, meta, tiles, back, *outs):
    rows, cols, count, place = lookup(meta)
    side = place(2) if mine else 1 - place(2)
    sign = 1 - 2 * side
    plan = ((LONG, 1), (SHORT, 1), (LONG, 0), (SHORT, 0))
    for out, (group, a) in zip(outs, plan):
        for n, (k, b) in enumerate(group):
            block = block_of(place, side, length, sign * k, a, b)
            live = count(block)
            low = jnp.zeros((TILE, TILE), F32)
            high = low
            for s in range(SLOTS):
                slot = block * SLOTS + s
                row = rows(slot)
                column = cols(slot)
                used = s < live
                tile = back[row // 2, pl.ds(pl.multiple_of((row % 2) * TILE, TILE), TILE), :]
                product = jnp.dot(tile, tiles[slot], preferred_element_type=F32)
                low += jnp.where(used & (column == 0), product, 0.0)
                high += jnp.where(used & (column != 0), product, 0.0)
            out[n, :TILE] = low.astype(BF16)
            out[n, TILE:] = high.astype(BF16)
    if mine:
        piece = jnp.sum(back[:, 2 * TILE :, :].astype(F32), axis=0).astype(BF16)
        for r in range(outs[4].shape[0]):
            outs[4][r] = piece


def backward_call(length, mine, meta, tiles, back):
    height, width = back.shape[1:]
    blocks = tiles.shape[0] // SLOTS
    shapes = [jax.ShapeDtypeStruct((len(LONG), 2 * TILE, width), BF16)] * 4
    if mine:
        shapes.append(jax.ShapeDtypeStruct((blocks, height - 2 * TILE, width), BF16))
    return pl.pallas_call(
        functools.partial(backward_kernel, length, mine),
        in_specs=[smem()] + [vmem()] * 2,
        out_specs=(vmem(),) * len(shapes),
        out_shape=tuple(shapes),
        compiler_params=params(),
        name="backward_near" if mine else "backward_far",
    )(meta, tiles, back)


def grad_kernel(parts, out):
    out[...] = jnp.broadcast_to(jnp.sum(parts[...].astype(F32), axis=0)[None], out.shape)


def grad_call(parts, replicas):
    return pl.pallas_call(
        grad_kernel,
        in_specs=[vmem()],
        out_specs=vmem(),
        out_shape=jax.ShapeDtypeStruct((replicas,) + parts.shape[1:], F32),
        compiler_params=params(),
        name="grad",
    )(parts)


def fold_kernel(one, two, three, four, own, keep, give):
    total = one[...].astype(F32) + two[...].astype(F32) + three[...].astype(F32)
    keep[...] = total[0] + four[0].astype(F32) + own[0].astype(F32)
    give[...] = total[1].astype(BF16)


def fold_call(parts, own):
    shape = own.shape[1:]
    return pl.pallas_call(
        fold_kernel,
        in_specs=[vmem()] * 5,
        out_specs=(vmem(), vmem()),
        out_shape=(jax.ShapeDtypeStruct(shape, F32), jax.ShapeDtypeStruct(shape, BF16)),
        compiler_params=params(),
        name="fold",
    )(*parts, own)


def final_kernel(keep, got, back_own, scale_row, pieces, grad_features, grad_weight):
    for c in range(back_own.shape[0] // TILE):
        here = slice(c * TILE, (c + 1) * TILE)
        value = keep[here, :] + got[here, :].astype(F32) + back_own[here, :].astype(F32)
        grad_features[here, :] = (value * scale_row[c : c + 1, :]).T.astype(BF16)
    replicas, height, width = pieces.shape
    halves = grad_weight.shape[1] // width
    rows = height // halves
    for r in range(replicas):
        for h in range(halves):
            grad_weight[r * rows : (r + 1) * rows, h * width : (h + 1) * width] = pieces[
                r, h * rows : (h + 1) * rows, :
            ]


def final_call(keep, got, back_own, scale_row, pieces):
    replicas, height, width = pieces.shape
    return pl.pallas_call(
        final_kernel,
        in_specs=[vmem()] * 5,
        out_specs=(vmem(), vmem()),
        out_shape=(
            jax.ShapeDtypeStruct(back_own.shape, BF16),
            jax.ShapeDtypeStruct((TILE, replicas * height * width // TILE), F32),
        ),
        compiler_params=params(),
        name="final",
    )(keep, got, back_own, scale_row, pieces)


SWAP = ((0, 1), (1, 0))


def body(features, tile_values, tile_rows, tile_cols, tile_count, weight, bias, cotangent):
    replicas = lax.axis_size("rep")
    length = lax.axis_size("zed")
    blocks = tile_count.shape[1]
    sub, width = features.shape
    row_tiles = sub * replicas // TILE
    place = [lax.axis_index(n).astype(jnp.int32).reshape(1, 1) for n in ("zed", "pair", "core")]
    meta = jnp.concatenate([tile_rows, tile_cols, tile_count, *place], axis=1)

    def along(value, k):
        moves = [
            (z * 2 + c, (z + (1 - 2 * c) * k) % length * 2 + c)
            for z in range(length)
            for c in range(2)
        ]
        return lax.ppermute(value, ("zed", "core"), moves)

    def swap(value, axis):
        return lax.ppermute(value, axis, SWAP)

    partner = swap(features, "pair")
    sibling = swap(features, "core")
    partial = degree_call(meta, tile_values, row_tiles)
    partner, partial = lax.optimization_barrier((partner, partial))
    own, two = join_call(features, partner, sibling, swap(partner, "core"))
    own, two, partial = lax.optimization_barrier((own, two, partial))
    near = [along(own if k < REACH else two, k) for k in range(1, REACH + 1)]
    parts = lax.all_to_all(
        partial.reshape(replicas, sub // TILE, TILE), "rep", 0, 0, tiled=True
    )
    scale_row, scale_col, spread = scale_call(parts, blocks)
    scales = lax.all_to_all(spread, ("zed", "pair", "core"), 0, 0, tiled=True)
    scales, near = lax.optimization_barrier((scales, near))
    far = [swap(value, "core") for value in near]
    sums = forward_call(length, meta, tile_values, scales, None, [own, *near], row_tiles)
    sums = forward_call(length, meta, tile_values, scales, sums, far, row_tiles)
    sums = lax.all_to_all(sums.reshape(replicas, sub, width), "rep", 0, 0, tiled=True)
    hidden, back_own, pay = dense_call(
        sums, features, scale_col, scale_row, weight, bias.reshape(1, -1), cotangent
    )
    back = lax.all_to_all(pay, "rep", 0, 0, tiled=True)

    far = backward_call(length, False, meta, tile_values, back)
    far = [swap(value, "core") for value in far]
    *near, piece = backward_call(length, True, meta, tile_values, back)
    sums = [n + f for n, f in zip(near, far)]
    sums[0], sums[1], piece = lax.optimization_barrier((sums[0], sums[1], piece))
    other = [swap(value, "pair") for value in sums[:2]]
    piece = lax.all_to_all(piece, ("zed", "pair", "core"), 0, 0, tiled=True)
    piece = grad_call(piece, replicas)
    reach = sums[2] + other[0]
    three, two = along(reach[:2], 3), along(reach[2:], 2)
    other[1], piece = lax.optimization_barrier((other[1], piece))
    piece = lax.all_to_all(piece, "rep", 0, 0, tiled=True)
    close = sums[3] + other[1]
    one, four = along(close[:2], 1), along(close[2:3], 4)
    keep, give = fold_call((one, two, three, four), close[3:])
    grad_features, grad_weight = final_call(
        keep, swap(give, "core"), back_own, scale_row, piece
    )
    return hidden, grad_features, grad_weight


def solution(mesh):
    rows, replicas = mesh.devices.shape
    fine = Mesh(
        mesh.devices.reshape(rows // 4, 2, 2, replicas), ("zed", "pair", "core", "rep")
    )
    whole = ("zed", "pair", "core", "rep")
    placed = (
        P(whole, None),
        P(whole, None, None),
        P(whole, None),
        P(whole, None),
        P(whole, None),
        P(),
        P(),
        P(whole, None),
    )
    return jax.shard_map(
        body,
        mesh=fine,
        in_specs=placed,
        out_specs=(P(whole, None), P(whole, None), P()),
        check_vma=False,
    )
```

```python
import functools

import jax
import jax.numpy as jnp
from jax import lax
from jax.experimental import pallas as pl
from jax.experimental.pallas import tpu as pltpu
from jax.sharding import Mesh, PartitionSpec as P

TILE = 128
SLOTS = 8
BF16 = jnp.bfloat16
F32 = jnp.float32
VMEM_BYTES = 16 * 1024 * 1024
DEGREE_BYTES = 50 * 1024 * 1024
REACH = 4


def params():
    return pltpu.CompilerParams(vmem_limit_bytes=VMEM_BYTES)


def vmem():
    return pl.BlockSpec(memory_space=pltpu.VMEM)


def smem():
    return pl.BlockSpec(memory_space=pltpu.SMEM)


def lookup(meta):
    slots = (meta.shape[1] - 3) * SLOTS // (2 * SLOTS + 1)
    blocks = slots // SLOTS

    def rows(slot):
        return meta[0, slot]

    def cols(slot):
        return meta[0, slots + slot]

    def count(block):
        return meta[0, 2 * slots + block]

    def place(axis):
        return meta[0, 2 * slots + blocks + axis]

    return rows, cols, count, place


def degree_kernel(chunks, meta, tiles, out, held, acc, sems):
    rows, _, count, _ = lookup(meta)
    row_tiles = out.shape[0]
    size = tiles.shape[0] // chunks
    copies = [
        pltpu.make_async_copy(
            tiles.at[pl.ds(c * size, size)], held.at[pl.ds(c * size, size)], sems.at[c]
        )
        for c in range(chunks)
    ]
    for copy in copies:
        copy.start()
    acc[...] = jnp.zeros_like(acc)
    ones = jnp.ones((16, TILE), BF16)
    for c in range(chunks):
        copies[c].wait()
        for block in range(c * size // SLOTS, (c + 1) * size // SLOTS):
            live = count(block)
            stack = held[block * SLOTS : (block + 1) * SLOTS].reshape(SLOTS * TILE, TILE)
            sums = lax.dot_general(
                ones, stack, (((1,), (1,)), ((), ())), preferred_element_type=F32
            )
            for s in range(SLOTS):
                row = jnp.where(s < live, rows(block * SLOTS + s), row_tiles)
                acc[row] += sums[:8, s * TILE : (s + 1) * TILE]
    for r in range(row_tiles):
        out[r : r + 1, :] = acc[r, 0:1, :]


def degree_call(meta, tiles, row_tiles, chunks=4):
    return pl.pallas_call(
        functools.partial(degree_kernel, chunks),
        in_specs=[smem(), pl.BlockSpec(memory_space=pl.ANY)],
        out_specs=vmem(),
        out_shape=jax.ShapeDtypeStruct((row_tiles, TILE), F32),
        scratch_shapes=[
            pltpu.VMEM(tiles.shape, BF16),
            pltpu.VMEM((row_tiles + 1, 8, TILE), F32),
            pltpu.SemaphoreType.DMA((chunks,)),
        ],
        compiler_params=pltpu.CompilerParams(vmem_limit_bytes=DEGREE_BYTES),
        name="degree",
    )(meta, tiles)


def join_kernel(one, two, three, four, out, half):
    for i, piece in enumerate((one, two, three, four)):
        out[i] = piece[...]
        if i < 2:
            half[i] = piece[...]


def join_call(*pieces):
    shape = pieces[0].shape
    return pl.pallas_call(
        join_kernel,
        in_specs=[vmem()] * 4,
        out_specs=(vmem(), vmem()),
        out_shape=(
            jax.ShapeDtypeStruct((4,) + shape, BF16),
            jax.ShapeDtypeStruct((2,) + shape, BF16),
        ),
        compiler_params=params(),
        name="join",
    )(*pieces)


def scale_kernel(parts, row_out, col_out, spread):
    degree = 1.0 + jnp.sum(parts[...], axis=0)
    scale = lax.rsqrt(degree)
    row_out[...] = scale
    for c in range(scale.shape[0]):
        here = slice(c * TILE, (c + 1) * TILE)
        col_out[here, :] = jnp.broadcast_to(scale[c : c + 1, :], (TILE, TILE)).T
    spread[...] = jnp.broadcast_to(scale[None], spread.shape)


def scale_call(parts, copies):
    halves = parts.shape[1]
    return pl.pallas_call(
        scale_kernel,
        in_specs=[vmem()],
        out_specs=(vmem(), vmem(), vmem()),
        out_shape=(
            jax.ShapeDtypeStruct((halves, TILE), F32),
            jax.ShapeDtypeStruct((halves * TILE, TILE), F32),
            jax.ShapeDtypeStruct((copies, halves, TILE), F32),
        ),
        compiler_params=params(),
        name="scale",
    )(parts)


def block_of(place, core, length, ahead, a, b):
    there = lax.rem(place(0) + ahead + length, length)
    return there * 4 + (place(1) ^ a) * 2 + (core ^ b)


def forward_kernel(length, first, meta, tiles, scales, *refs):
    rows, cols, count, place = lookup(meta)
    core = place(2)
    sign = 1 - 2 * core
    if first:
        sources, (out, scaled) = refs[:-2], refs[-2:]
        acc = out
        work = [(sources[0], i, core, 0) for i in range(4)]
        for k in range(1, REACH + 1):
            work += [(sources[k], i, core, -sign * k) for i in range(sources[k].shape[0])]
    else:
        before, sources, (out, scaled, acc) = refs[0], refs[1:-3], refs[-3:]
        work = []
        for k in range(1, REACH + 1):
            piece = sources[k - 1]
            work += [(piece, i, 1 - core, sign * k) for i in range(piece.shape[0])]
    row_tiles = acc.shape[0] - 1
    acc[...] = jnp.zeros_like(acc)
    for n, (source, i, side, ahead) in enumerate(work):
        block = block_of(place, side, length, ahead, i % 2, i // 2)
        live = count(block)
        for c in range(2):
            column = jnp.broadcast_to(scales[block, c : c + 1, :], (TILE, TILE)).T
            plain = source[i, c * TILE : (c + 1) * TILE, :].astype(F32)
            scaled[n, c] = (column * plain).astype(BF16)
        for s in range(SLOTS):
            slot = block * SLOTS + s
            product = jnp.dot(
                tiles[slot], scaled[n, cols(slot)], preferred_element_type=F32
            )
            row = jnp.where(s < live, rows(slot), row_tiles)
            acc[row] += product
    if not first:
        out[...] = (before[:row_tiles] + acc[:row_tiles]).astype(BF16)


def forward_call(length, meta, tiles, scales, before, sources, row_tiles):
    blocks = scales.shape[0]
    width = sources[0].shape[2]
    first = before is None
    total = (row_tiles + 1, TILE, width)
    given = list(sources) if first else [before, *sources]
    scratch = [pltpu.VMEM((blocks, 2, TILE, width), BF16)]
    if first:
        shape = jax.ShapeDtypeStruct(total, F32)
    else:
        shape = jax.ShapeDtypeStruct((row_tiles, TILE, width), BF16)
        scratch.append(pltpu.VMEM(total, F32))
    return pl.pallas_call(
        functools.partial(forward_kernel, length, first),
        in_specs=[smem()] + [vmem()] * (2 + len(given)),
        out_specs=vmem(),
        out_shape=shape,
        scratch_shapes=scratch,
        compiler_params=params(),
        name="forward_near" if first else "forward_far",
    )(meta, tiles, scales, *given)


def dense_kernel(parts, features, scale_col, scale_row, weight, bias, cotangent, hidden, back_own, pay):
    sub = features.shape[0]
    replicas = parts.shape[0]
    column = scale_col[...]
    total = (column * features[...].astype(F32)).astype(BF16).astype(F32)
    for r in range(replicas):
        total += parts[r].astype(F32)
    agg_b = (column * total).astype(BF16)
    w = weight[...]
    v = jnp.dot(agg_b, w, preferred_element_type=F32) + bias[...]
    root = 0.7978845608028654
    square = v * v
    t = jnp.tanh(root * (v + 0.044715 * (square * v)))
    cdf = 0.5 * (1.0 + t)
    hidden[...] = (v * cdf).astype(BF16)
    slope = cdf + 0.5 * v * ((1.0 - t) * (1.0 + t)) * (root * (1.0 + (3 * 0.044715) * square))
    dpre = (cotangent[...].astype(F32) * slope).astype(BF16)
    grad = lax.dot_general(agg_b, dpre, (((0,), (0,)), ((), ())), preferred_element_type=F32)
    back = lax.dot_general(w, dpre, (((1,), (1,)), ((), ())), preferred_element_type=F32)
    for c in range(sub // TILE):
        here = slice(c * TILE, (c + 1) * TILE)
        piece = (back[:, here] * scale_row[c : c + 1, :]).astype(BF16)
        back_own[here, :] = piece
        for r in range(replicas):
            pay[r, here, :] = piece
    grad_b = grad.astype(BF16)
    rows = grad.shape[0] // replicas
    for r in range(replicas):
        for h in range(grad.shape[1] // TILE):
            pay[r, sub + h * rows : sub + (h + 1) * rows, :] = grad_b[
                r * rows : (r + 1) * rows, h * TILE : (h + 1) * TILE
            ]


def dense_call(parts, features, scale_col, scale_row, weight, bias, cotangent):
    sub, width = features.shape
    replicas = parts.shape[0]
    hid = weight.shape[1]
    extra = width // replicas * (hid // TILE)
    return pl.pallas_call(
        dense_kernel,
        in_specs=[vmem()] * 7,
        out_specs=(vmem(), vmem(), vmem()),
        out_shape=(
            jax.ShapeDtypeStruct((sub, hid), BF16),
            jax.ShapeDtypeStruct((sub, width), BF16),
            jax.ShapeDtypeStruct((replicas, sub + extra, width), BF16),
        ),
        compiler_params=params(),
        name="dense",
    )(parts, features, scale_col, scale_row, weight, bias, cotangent)


LONG = ((3, 0), (3, 1), (2, 0), (2, 1), (4, 0))
SHORT = ((1, 0), (1, 1), (0, 0))


def backward_kernel(length, mine, meta, tiles, back, *outs):
    rows, cols, count, place = lookup(meta)
    side = place(2) if mine else 1 - place(2)
    sign = 1 - 2 * side
    plan = ((LONG, 1), (SHORT, 1), (LONG, 0), (SHORT, 0))
    for out, (group, a) in zip(outs, plan):
        for n, (k, b) in enumerate(group):
            block = block_of(place, side, length, sign * k, a, b)
            live = count(block)
            low = jnp.zeros((TILE, TILE), F32)
            high = low
            for s in range(SLOTS):
                slot = block * SLOTS + s
                row = rows(slot)
                column = cols(slot)
                used = s < live
                tile = back[row // 2, pl.ds(pl.multiple_of((row % 2) * TILE, TILE), TILE), :]
                product = jnp.dot(tile, tiles[slot], preferred_element_type=F32)
                low += jnp.where(used & (column == 0), product, 0.0)
                high += jnp.where(used & (column != 0), product, 0.0)
            out[n, :TILE] = low.astype(BF16)
            out[n, TILE:] = high.astype(BF16)
    if mine:
        piece = jnp.sum(back[:, 2 * TILE :, :].astype(F32), axis=0).astype(BF16)
        for r in range(outs[4].shape[0]):
            outs[4][r] = piece


def backward_call(length, mine, meta, tiles, back):
    height, width = back.shape[1:]
    blocks = tiles.shape[0] // SLOTS
    shapes = [
        jax.ShapeDtypeStruct((len(group), 2 * TILE, width), BF16)
        for group in (LONG, SHORT, LONG, SHORT)
    ]
    if mine:
        shapes.append(jax.ShapeDtypeStruct((blocks, height - 2 * TILE, width), BF16))
    return pl.pallas_call(
        functools.partial(backward_kernel, length, mine),
        in_specs=[smem()] + [vmem()] * 2,
        out_specs=(vmem(),) * len(shapes),
        out_shape=tuple(shapes),
        compiler_params=params(),
        name="backward_near" if mine else "backward_far",
    )(meta, tiles, back)


def grad_kernel(parts, out):
    out[...] = jnp.broadcast_to(jnp.sum(parts[...].astype(F32), axis=0)[None], out.shape)


def grad_call(parts, replicas):
    return pl.pallas_call(
        grad_kernel,
        in_specs=[vmem()],
        out_specs=vmem(),
        out_shape=jax.ShapeDtypeStruct((replicas,) + parts.shape[1:], F32),
        compiler_params=params(),
        name="grad",
    )(parts)


def fold_kernel(one, two, three, four, own, keep, give):
    total = one[...].astype(F32) + two[...].astype(F32) + three[...].astype(F32)
    keep[...] = total[0] + four[0].astype(F32) + own[0].astype(F32)
    give[...] = total[1].astype(BF16)


def fold_call(parts, own):
    shape = own.shape[1:]
    return pl.pallas_call(
        fold_kernel,
        in_specs=[vmem()] * 5,
        out_specs=(vmem(), vmem()),
        out_shape=(jax.ShapeDtypeStruct(shape, F32), jax.ShapeDtypeStruct(shape, BF16)),
        compiler_params=params(),
        name="fold",
    )(*parts, own)


def final_kernel(keep, got, back_own, scale_row, pieces, grad_features, grad_weight):
    for c in range(back_own.shape[0] // TILE):
        here = slice(c * TILE, (c + 1) * TILE)
        value = keep[here, :] + got[here, :].astype(F32) + back_own[here, :].astype(F32)
        grad_features[here, :] = (value * scale_row[c : c + 1, :]).T.astype(BF16)
    replicas, height, width = pieces.shape
    halves = grad_weight.shape[1] // width
    rows = height // halves
    for r in range(replicas):
        for h in range(halves):
            grad_weight[r * rows : (r + 1) * rows, h * width : (h + 1) * width] = pieces[
                r, h * rows : (h + 1) * rows, :
            ]


def final_call(keep, got, back_own, scale_row, pieces):
    replicas, height, width = pieces.shape
    return pl.pallas_call(
        final_kernel,
        in_specs=[vmem()] * 5,
        out_specs=(vmem(), vmem()),
        out_shape=(
            jax.ShapeDtypeStruct(back_own.shape, BF16),
            jax.ShapeDtypeStruct((TILE, replicas * height * width // TILE), F32),
        ),
        compiler_params=params(),
        name="final",
    )(keep, got, back_own, scale_row, pieces)


SWAP = ((0, 1), (1, 0))


def body(features, tile_values, tile_rows, tile_cols, tile_count, weight, bias, cotangent):
    replicas = lax.axis_size("rep")
    length = lax.axis_size("zed")
    blocks = tile_count.shape[1]
    sub, width = features.shape
    row_tiles = sub * replicas // TILE
    place = [lax.axis_index(n).astype(jnp.int32).reshape(1, 1) for n in ("zed", "pair", "core")]
    meta = jnp.concatenate([tile_rows, tile_cols, tile_count, *place], axis=1)

    def along(value, k):
        moves = [
            (z * 2 + c, (z + (1 - 2 * c) * k) % length * 2 + c)
            for z in range(length)
            for c in range(2)
        ]
        return lax.ppermute(value, ("zed", "core"), moves)

    def swap(value, axis):
        return lax.ppermute(value, axis, SWAP)

    partner = swap(features, "pair")
    sibling = swap(features, "core")
    partial = degree_call(meta, tile_values, row_tiles)
    partner, partial = lax.optimization_barrier((partner, partial))
    own, two = join_call(features, partner, sibling, swap(partner, "core"))
    own, two, partial = lax.optimization_barrier((own, two, partial))
    near = [along(own if k < REACH else two, k) for k in range(1, REACH + 1)]
    parts = lax.all_to_all(
        partial.reshape(replicas, sub // TILE, TILE), "rep", 0, 0, tiled=True
    )
    scale_row, scale_col, spread = scale_call(parts, blocks)
    scales = lax.all_to_all(spread, ("zed", "pair", "core"), 0, 0, tiled=True)
    scales, near = lax.optimization_barrier((scales, near))
    far = [swap(value, "core") for value in near]
    sums = forward_call(length, meta, tile_values, scales, None, [own, *near], row_tiles)
    sums = forward_call(length, meta, tile_values, scales, sums, far, row_tiles)
    sums = lax.all_to_all(sums.reshape(replicas, sub, width), "rep", 0, 0, tiled=True)
    hidden, back_own, pay = dense_call(
        sums, features, scale_col, scale_row, weight, bias.reshape(1, -1), cotangent
    )
    back = lax.all_to_all(pay, "rep", 0, 0, tiled=True)

    far = backward_call(length, False, meta, tile_values, back)
    far = [swap(value, "core") for value in far]
    *near, piece = backward_call(length, True, meta, tile_values, back)
    sums = [n + f for n, f in zip(near, far)]
    sums[0], sums[1], piece = lax.optimization_barrier((sums[0], sums[1], piece))
    other = [swap(value, "pair") for value in sums[:2]]
    piece = lax.all_to_all(piece, ("zed", "pair", "core"), 0, 0, tiled=True)
    piece = grad_call(piece, replicas)
    reach = sums[2] + other[0]
    three, two, four = along(reach[:2], 3), along(reach[2:4], 2), along(reach[4:], 4)
    other[1], piece = lax.optimization_barrier((other[1], piece))
    piece = lax.all_to_all(piece, "rep", 0, 0, tiled=True)
    close = sums[3] + other[1]
    one = along(close[:2], 1)
    keep, give = fold_call((one, two, three, four), close[2:])
    grad_features, grad_weight = final_call(
        keep, swap(give, "core"), back_own, scale_row, piece
    )
    return hidden, grad_features, grad_weight


def solution(mesh):
    rows, replicas = mesh.devices.shape
    fine = Mesh(
        mesh.devices.reshape(rows // 4, 2, 2, replicas), ("zed", "pair", "core", "rep")
    )
    whole = ("zed", "pair", "core", "rep")
    placed = (
        P(whole, None),
        P(whole, None, None),
        P(whole, None),
        P(whole, None),
        P(whole, None),
        P(),
        P(),
        P(whole, None),
    )
    return jax.shard_map(
        body,
        mesh=fine,
        in_specs=placed,
        out_specs=(P(whole, None), P(whole, None), P()),
        check_vma=False,
    )
```
